256 devices in a mesh: replica: 8 (over y, x_hi), fsdp: 32 (over x_lo, z, core).
Axes of the slice: x: 4 (x_hi: 2, x_lo: 2; x = x_hi * 2 + x_lo), y: 4, z: 8, core: 2. Of those that a mesh axis runs over, the one named last changes fastest.
Arguments:
- local_params: bfloat16 [8, 4096, 14336], P('replica', 'fsdp'), may hold values from -6 to 6
- outer_params: float32 [32, 32, 8, 14336], P('fsdp', None, None, 'replica'), may hold values from -6 to 6
- outer_momentum: float32 [32, 32, 8, 14336], P('fsdp', None, None, 'replica'), may hold values from -3 to 3
- block_lengths: int32 [32, 24], replicated, may hold values from 1 to 8, 128 in all within a row
- block_owners: int32 [32, 32], replicated, may hold values from 0 to 31, each once within a row
Outputs:
- new_outer: float32 [32, 32, 8, 14336], P('fsdp', None, None, 'replica')
- new_momentum: float32 [32, 32, 8, 14336], P('fsdp', None, None, 'replica')
- new_params: bfloat16 [4096, 14336], P('fsdp')
The draws below stay inside these ranges and needn't reach their ends.
Inputs may be any that keep to these rules, and one draw needn't show every extreme that they name: `block_lengths`: each row sums to 128 and has a block of exactly 8 rows. `block_owners`: each row is a permutation; only its first 24 entries name owners, so an owner gets at most one block from each index.
All inputs are finite; a program needn't handle non-finite values.
Results may differ from the reference program's by a relative error of at most 0.014.
Values may be sent and summed in bfloat16 or wider, within the bound.
No kernel may reach another device: no remote copies, remote signals or barrier semaphores. Data moves between devices by JAX's collectives and lax.ppermute only.
A program may use at most 128 MiB of HBM per device.

```python
import math
import jax
import jax.numpy as jnp
import numpy as np

FF = 14336
ROWS_DEV = 128
REPLICAS = 8
FRAG = 4096
CAP = 8
NBLK = 24
N_FSDP = 32


def levels(own_key, extent, split, smallest, high):
    def one(position, parts):
        steps = jax.random.uniform(jax.random.fold_in(jax.random.fold_in(own_key, 6), position), (parts,), jnp.float32, smallest / len(split), high / len(split))
        return jnp.repeat(jnp.exp(steps), extent[position] // parts).reshape((-1,) + (1,) * (len(extent) - position - 1))

    loudness = one(*split[0])
    for cut in split[1:]:
        loudness = loudness * one(*cut)
    return loudness


def length_profile(number_of, total, bound, skew):
    weights = [(1 << 20) // math.isqrt(standing ** skew) + 1 for standing in range(2, number_of + 1)]
    rest, given = total - bound - (number_of - 1), [1] * (number_of - 1)
    while rest > 0:
        movable = [i for i in range(number_of - 1) if given[i] < bound]
        mass, left = sum([weights[i] for i in movable]), rest
        for i in movable:
            extra = min(bound - given[i], max(1, left * weights[i] // mass), rest)
            given[i] = given[i] + extra
            rest = rest - extra
    return np.array([bound] + given)


def uneven_parts(stream_key, number_of, total, bound, slope):
    if number_of == 2:
        one = jax.random.randint(stream_key, (), max(1, total - bound), min(bound, total - 1) + 1)
        return jnp.stack([one, total - one])
    lengths = jnp.asarray(length_profile(number_of, total, bound, slope), jnp.int32)
    twos = (number_of - 1) // 2
    donor, sink = lengths[1:1 + 2 * twos:2], lengths[2:2 + 2 * twos:2]
    room = jnp.minimum(donor - 1, bound - sink)
    passed = jax.random.randint(jax.random.fold_in(stream_key, 1), (twos,), 0, 1 << 20) % (room + 1)
    lengths = lengths.at[1:1 + 2 * twos:2].set(donor - passed).at[2:2 + 2 * twos:2].set(sink + passed)
    return lengths[jax.random.permutation(jax.random.fold_in(stream_key, 2), number_of)]


def gaussian(own_key, extent, scale, most, split=(), held_as=jnp.bfloat16):
    values = scale * jax.random.normal(own_key, extent, jnp.float32)
    if split:
        values = values * levels(own_key, extent, split, -0.22, 0.18)
    return jnp.clip(values, -most, most).astype(held_as)


def setup_inputs(seed: int = 0) -> dict:
    splits = jax.random.split(jax.random.key(seed), 6)
    local_params = gaussian(splits[0], (REPLICAS, FRAG, FF), 1.0, 6.0, ((0, 8), (1, 32)))
    outer_params = gaussian(splits[1], (N_FSDP, N_FSDP, CAP, FF), 1.0, 6.0, ((0, 32), (3, 8)), jnp.float32)
    outer_momentum = gaussian(splits[2], (N_FSDP, N_FSDP, CAP, FF), 0.5, 3.0, ((0, 32), (3, 8)), jnp.float32)
    block_lengths = jax.vmap(lambda own: uneven_parts(own, NBLK, ROWS_DEV, CAP, 0))(jax.random.split(splits[3], N_FSDP)).reshape((N_FSDP, NBLK)).astype(jnp.int32)
    block_owners = jax.vmap(lambda own: jax.random.permutation(own, N_FSDP))(jax.random.split(splits[4], N_FSDP)).reshape((N_FSDP, N_FSDP)).astype(jnp.int32)
    return {"local_params": local_params, "outer_params": outer_params, "outer_momentum": outer_momentum, "block_lengths": block_lengths, "block_owners": block_owners}


outer_rate = 0.7
momentum_decay = 0.9


def tables(block_lengths, block_owners, owner_count):
    block_count = block_lengths.shape[1]
    offsets = jnp.cumsum(block_lengths, axis=1).astype(jnp.int32) - block_lengths
    heads = block_owners[:, :block_count]
    owner_ids = jnp.arange(owner_count, dtype=jnp.int32)
    match = (heads[:, :, None] == owner_ids[None, None, :]).astype(jnp.int32)
    counts = jnp.sum(match * block_lengths[:, :, None], axis=1).astype(jnp.int32)
    starts = jnp.sum(match * offsets[:, :, None], axis=1).astype(jnp.int32)
    return offsets, counts, starts


def locate(offsets, block_lengths, block_owners, row_count):
    row_ids = jnp.arange(row_count, dtype=jnp.int32)
    block_ends = offsets + block_lengths
    block_of_row = jnp.sum((block_ends[:, None, :] <= row_ids[None, :, None]).astype(jnp.int32), axis=2).astype(jnp.int32)
    owner_of_row = jnp.take_along_axis(block_owners, block_of_row, axis=1)
    slot_of_row = row_ids[None, :] - jnp.take_along_axis(offsets, block_of_row, axis=1)
    return owner_of_row.astype(jnp.int32), slot_of_row.astype(jnp.int32)


def reference(local_params, outer_params, outer_momentum, block_lengths, block_owners):
    summed_params = local_params[0].astype(jnp.float32)
    for group in range(1, REPLICAS):
        summed_params = summed_params + local_params[group].astype(jnp.float32)
    mean_params = summed_params / REPLICAS
    offsets, counts, starts = tables(block_lengths, block_owners, N_FSDP)
    slot_ids = jnp.arange(CAP, dtype=jnp.int32)
    source_ids = jnp.arange(N_FSDP, dtype=jnp.int32)
    gather_rows = source_ids[None, :, None] * ROWS_DEV + starts.T[:, :, None] + slot_ids[None, None, :]
    live_slots = slot_ids[None, None, :] < counts.T[:, :, None]
    gathered = jnp.take(mean_params, gather_rows.reshape(-1), axis=0, mode="clip").reshape(N_FSDP, N_FSDP, CAP, FF)
    pseudo_grad = jnp.where(live_slots[..., None], outer_params - gathered, jnp.float32(0.0))
    new_momentum = momentum_decay * outer_momentum + pseudo_grad
    new_outer = outer_params - outer_rate * (pseudo_grad + momentum_decay * new_momentum)
    owner_of_row, slot_of_row = locate(offsets, block_lengths, block_owners, ROWS_DEV)
    flat_index = (owner_of_row * N_FSDP + source_ids[:, None]) * CAP + slot_of_row
    rounded = new_outer.astype(jnp.bfloat16).reshape(N_FSDP * N_FSDP * CAP, FF)
    new_params = jnp.take(rounded, flat_index.reshape(-1), axis=0, mode="clip")
    return new_outer, new_momentum, new_params
```

```python
import jax
import jax.numpy as jnp
from jax import lax
from jax.sharding import PartitionSpec as P

outer_rate = 0.7
momentum_decay = 0.9


def tables(block_lengths, block_owners, owner_count):
    block_count = block_lengths.shape[1]
    block_ids = jnp.arange(block_count, dtype=jnp.int32)
    before = (block_ids[None, :] < block_ids[:, None]).astype(jnp.int32)
    offsets = jnp.sum(before[None] * block_lengths[:, None, :], axis=2)
    heads = block_owners[:, :block_count]
    owner_ids = jnp.arange(owner_count, dtype=jnp.int32)
    match = (heads[:, :, None] == owner_ids[None, None, :]).astype(jnp.int32)
    counts = jnp.sum(match * block_lengths[:, :, None], axis=1)
    starts = jnp.sum(match * offsets[:, :, None], axis=1)
    return counts, starts


def body(local_params, outer_params, outer_momentum, block_lengths, block_owners):
    fsdp_count = lax.axis_size("fsdp")
    group_count = lax.axis_size("replica")
    my_index = lax.axis_index("fsdp")
    own_rows = local_params[0]
    row_count = own_rows.shape[0]
    slots = outer_params.shape[2]
    columns = outer_params.shape[3]
    summed = lax.psum_scatter(own_rows, "replica", scatter_dimension=1, tiled=True)

    counts, starts = tables(block_lengths, block_owners, fsdp_count)
    slot_ids = jnp.arange(slots, dtype=jnp.int32)
    row_ids = jnp.arange(row_count, dtype=jnp.int32)
    my_starts = lax.dynamic_index_in_dim(starts, my_index, 0, keepdims=False)
    my_counts = lax.dynamic_index_in_dim(counts, my_index, 0, keepdims=False)
    incoming = lax.dynamic_index_in_dim(counts, my_index, 1, keepdims=False)
    live_in = slot_ids[None, :] < incoming[:, None]
    row_of_slot = jnp.where(
        slot_ids[None, :] < my_counts[:, None], my_starts[:, None] + slot_ids[None, :], -1
    ).reshape(-1)
    pick = (row_of_slot[:, None] == row_ids[None, :]).astype(own_rows.dtype)

    packed = jnp.dot(pick, summed, preferred_element_type=jnp.float32).astype(own_rows.dtype)
    arrived = lax.all_to_all(
        packed.reshape(fsdp_count, slots, columns), "fsdp", split_axis=0, concat_axis=0, tiled=True
    ).astype(jnp.float32)
    outer_here = outer_params[0]
    pseudo_grad = jnp.where(
        live_in[:, :, None], outer_here - arrived / group_count, jnp.float32(0.0)
    )
    fresh_momentum = momentum_decay * outer_momentum[0] + pseudo_grad
    fresh_outer = outer_here - outer_rate * (pseudo_grad + momentum_decay * fresh_momentum)
    returned = lax.all_to_all(
        fresh_outer.astype(jnp.bfloat16), "fsdp", split_axis=0, concat_axis=0, tiled=True
    )
    rows = lax.dot_general(
        pick,
        returned.reshape(fsdp_count * slots, columns),
        (((0,), (0,)), ((), ())),
        preferred_element_type=jnp.float32,
    ).astype(jnp.bfloat16)
    fresh_rows = lax.all_gather(rows, "replica", axis=1, tiled=True)
    return (fresh_outer[None], fresh_momentum[None], fresh_rows)


def solution(mesh):
    in_specs = (
        P("replica", "fsdp", None),
        P("fsdp", None, None, "replica"),
        P("fsdp", None, None, "replica"),
        P(),
        P(),
    )
    out_specs = (
        P("fsdp", None, None, "replica"),
        P("fsdp", None, None, "replica"),
        P("fsdp", None),
    )
    return jax.shard_map(body, mesh=mesh, in_specs=in_specs, out_specs=out_specs, check_vma=False)
```

```python
import functools

import jax
import jax.numpy as jnp
from jax import lax
from jax.experimental import pallas as pl
from jax.experimental.pallas import tpu as pltpu
from jax.sharding import PartitionSpec as P

outer_rate = 0.7
momentum_decay = 0.9
pull = outer_rate * (1.0 + momentum_decay)
keep = 1.0 - pull
drag = outer_rate * momentum_decay * momentum_decay


def tables(block_lengths, block_owners, owner_count):
    block_count = block_lengths.shape[1]
    block_ids = jnp.arange(block_count, dtype=jnp.int32)
    before = (block_ids[None, :] < block_ids[:, None]).astype(jnp.int32)
    offsets = jnp.sum(before[None] * block_lengths[:, None, :], axis=2)
    heads = block_owners[:, :block_count]
    owner_ids = jnp.arange(owner_count, dtype=jnp.int32)
    match = (heads[:, :, None] == owner_ids[None, None, :]).astype(jnp.int32)
    counts = jnp.sum(match * block_lengths[:, :, None], axis=1)
    starts = jnp.sum(match * offsets[:, :, None], axis=1)
    return counts, starts


def split_columns(rows, group_count):
    row_count, width = rows.shape
    columns = width // group_count

    def kernel(rows_ref, *refs):
        outs, sems = refs[:group_count], refs[group_count]
        me = lax.axis_index("replica")
        copies = []
        for k in range(group_count):
            to = lax.rem(me + k, group_count)
            copies.append(
                pltpu.make_async_copy(
                    rows_ref.at[:, pl.ds(pl.multiple_of(to * columns, 128), columns)],
                    outs[k],
                    sems.at[k],
                )
            )
        for copy in copies:
            copy.start()
        for copy in copies:
            copy.wait()

    return pl.pallas_call(
        kernel,
        out_shape=[jax.ShapeDtypeStruct((row_count, columns), rows.dtype)] * group_count,
        in_specs=[pl.BlockSpec(memory_space=pl.ANY)],
        out_specs=[pl.BlockSpec(memory_space=pl.ANY)] * group_count,
        scratch_shapes=[pltpu.SemaphoreType.DMA((group_count,))],
        cost_estimate=pl.CostEstimate(flops=0, bytes_accessed=4 * row_count * width, transcendentals=0),
        name="split_columns",
    )(rows)


def join_columns(chunks):
    group_count = len(chunks)
    row_count, columns = chunks[0].shape

    def kernel(*refs):
        ins, out, sems = refs[:group_count], refs[group_count], refs[group_count + 1]
        me = lax.axis_index("replica")
        copies = []
        for k in range(group_count):
            come = lax.rem(me + group_count - k, group_count)
            copies.append(
                pltpu.make_async_copy(
                    ins[k],
                    out.at[:, pl.ds(pl.multiple_of(come * columns, 128), columns)],
                    sems.at[k],
                )
            )
        for copy in copies:
            copy.start()
        for copy in copies:
            copy.wait()

    return pl.pallas_call(
        kernel,
        out_shape=jax.ShapeDtypeStruct((row_count, group_count * columns), chunks[0].dtype),
        in_specs=[pl.BlockSpec(memory_space=pl.ANY)] * group_count,
        out_specs=pl.BlockSpec(memory_space=pl.ANY),
        scratch_shapes=[pltpu.SemaphoreType.DMA((group_count,))],
        cost_estimate=pl.CostEstimate(
            flops=0, bytes_accessed=4 * row_count * columns * group_count, transcendentals=0
        ),
        name="join_columns",
    )(*chunks)


def fresh_and_packed(parts, base, pick, group_count):
    row_count, columns = parts[0].shape
    slot_count = pick.shape[0]
    width = 256

    def kernel(*refs):
        part_refs = refs[: len(parts)]
        base_ref, pick_ref, rows_ref, slots_ref = refs[len(parts) :]
        total = part_refs[0][...].astype(jnp.float32)
        for ref in part_refs[1:]:
            total = total + ref[...].astype(jnp.float32)
        own_base = lax.dot_general(
            pick_ref[...],
            base_ref[...],
            (((0,), (0,)), ((), ())),
            preferred_element_type=jnp.float32,
        )
        rows_ref[...] = (own_base + (pull / group_count) * total).astype(rows_ref.dtype)
        slots_ref[...] = jnp.dot(
            pick_ref[...], total.astype(pick_ref.dtype), preferred_element_type=jnp.float32
        ).astype(slots_ref.dtype)

    block = pl.BlockSpec((row_count, width), lambda i: (0, i))
    slot_block = pl.BlockSpec((slot_count, width), lambda i: (0, i))
    return pl.pallas_call(
        kernel,
        grid=(columns // width,),
        out_shape=[
            jax.ShapeDtypeStruct((row_count, columns), jnp.bfloat16),
            jax.ShapeDtypeStruct((slot_count, columns), jnp.bfloat16),
        ],
        in_specs=[block] * len(parts)
        + [slot_block, pl.BlockSpec((slot_count, row_count), lambda i: (0, 0))],
        out_specs=[block, slot_block],
        cost_estimate=pl.CostEstimate(
            flops=4 * row_count * slot_count * columns,
            bytes_accessed=2 * columns * (row_count * (len(parts) + 1) + 2 * slot_count),
            transcendentals=0,
        ),
        name="fresh_and_packed",
    )(*parts, base, pick)


def body(local_params, outer_params, outer_momentum, block_lengths, block_owners):
    fsdp_count = lax.axis_size("fsdp")
    group_count = lax.axis_size("replica")
    my_index = lax.axis_index("fsdp")
    own_rows = local_params[0]
    row_count = own_rows.shape[0]
    slots = outer_params.shape[2]
    columns = outer_params.shape[3]
    outer_here = outer_params[0]
    momentum_here = outer_momentum[0]

    def ahead(array, k):
        return lax.ppermute(
            array, "replica", [(i, (i + k) % group_count) for i in range(group_count)]
        )

    chunks = split_columns(own_rows, group_count)
    parts = [chunks[0]] + [ahead(chunks[k], k) for k in range(1, group_count)]

    base = (keep * outer_here - drag * momentum_here).astype(jnp.bfloat16)
    own_base = lax.all_to_all(base, "fsdp", split_axis=0, concat_axis=0, tiled=True)

    counts, starts = tables(block_lengths, block_owners, fsdp_count)
    slot_ids = jnp.arange(slots, dtype=jnp.int32)
    row_ids = jnp.arange(row_count, dtype=jnp.int32)
    my_starts = lax.dynamic_index_in_dim(starts, my_index, 0, keepdims=False)
    my_counts = lax.dynamic_index_in_dim(counts, my_index, 0, keepdims=False)
    incoming = lax.dynamic_index_in_dim(counts, my_index, 1, keepdims=False)
    live_in = slot_ids[None, :] < incoming[:, None]
    row_of_slot = jnp.where(
        slot_ids[None, :] < my_counts[:, None], my_starts[:, None] + slot_ids[None, :], -1
    ).reshape(-1)
    pick = (row_of_slot[:, None] == row_ids[None, :]).astype(own_rows.dtype)

    rows, packed = fresh_and_packed(
        parts, own_base.reshape(fsdp_count * slots, columns), pick, group_count
    )
    gathered = [rows] + [ahead(rows, k) for k in range(1, group_count)]
    arrived = lax.all_to_all(
        packed.reshape(fsdp_count, slots, columns), "fsdp", split_axis=0, concat_axis=0, tiled=True
    ).astype(jnp.float32)
    pseudo_grad = jnp.where(
        live_in[:, :, None], outer_here - arrived / group_count, jnp.float32(0.0)
    )
    fresh_momentum = momentum_decay * momentum_here + pseudo_grad
    fresh_outer = outer_here - outer_rate * (pseudo_grad + momentum_decay * fresh_momentum)
    return (fresh_outer[None], fresh_momentum[None], join_columns(gathered))


def solution(mesh):
    in_specs = (
        P("replica", "fsdp", None),
        P("fsdp", None, None, "replica"),
        P("fsdp", None, None, "replica"),
        P(),
        P(),
    )
    out_specs = (
        P("fsdp", None, None, "replica"),
        P("fsdp", None, None, "replica"),
        P("fsdp", None),
    )
    return jax.shard_map(body, mesh=mesh, in_specs=in_specs, out_specs=out_specs, check_vma=False)
```

```python
import jax
import jax.numpy as jnp
from jax import lax
from jax.experimental import pallas as pl
from jax.experimental.pallas import tpu as pltpu
from jax.sharding import PartitionSpec as P

outer_rate = 0.7
momentum_decay = 0.9
PACE = 1150000000000
pull = outer_rate * (1.0 + momentum_decay)
keep = 1.0 - pull
drag = outer_rate * momentum_decay * momentum_decay

STEPS = [(0, 0), (1, 0), (3, 0), (2, 0), (0, 1), (1, 1), (3, 1), (2, 1)]


def place(me, step):
    y, x = me // 2, me % 2
    return ((y + step[0]) % 4) * 2 + (x + step[1]) % 2


def place_traced(me, step):
    y, x = lax.div(me, 2), lax.rem(me, 2)
    return lax.rem(y + step[0], 4) * 2 + lax.rem(x + step[1], 2)


def send(array, step):
    return lax.ppermute(array, "replica", [(i, place(i, step)) for i in range(8)])


def tables(block_lengths, block_owners, owner_count):
    block_count = block_lengths.shape[1]
    block_ids = jnp.arange(block_count, dtype=jnp.int32)
    before = (block_ids[None, :] < block_ids[:, None]).astype(jnp.int32)
    offsets = jnp.sum(before[None] * block_lengths[:, None, :], axis=2)
    heads = block_owners[:, :block_count]
    owner_ids = jnp.arange(owner_count, dtype=jnp.int32)
    match = (heads[:, :, None] == owner_ids[None, None, :]).astype(jnp.int32)
    counts = jnp.sum(match * block_lengths[:, :, None], axis=1)
    starts = jnp.sum(match * offsets[:, :, None], axis=1)
    return counts, starts


def split_columns(rows):
    row_count, width = rows.shape
    parts = len(STEPS)
    columns = width // parts

    def kernel(rows_ref, *refs):
        outs, sems = refs[:parts], refs[parts]
        me = lax.axis_index("replica")
        copies = []
        for k, step in enumerate(STEPS):
            to = place_traced(me, step)
            copies.append(
                pltpu.make_async_copy(
                    rows_ref.at[:, pl.ds(pl.multiple_of(to * columns, 128), columns)],
                    outs[k],
                    sems.at[k],
                )
            )
        for copy in copies:
            copy.start()
        for copy in copies:
            copy.wait()

    chunks = pl.pallas_call(
        kernel,
        out_shape=[jax.ShapeDtypeStruct((row_count, columns), rows.dtype)] * parts,
        in_specs=[pl.BlockSpec(memory_space=pltpu.HBM)],
        out_specs=[pl.BlockSpec(memory_space=pltpu.VMEM)] * parts,
        scratch_shapes=[pltpu.SemaphoreType.DMA((parts,))],
        cost_estimate=pl.CostEstimate(
            flops=0, bytes_accessed=4 * row_count * width, transcendentals=0
        ),
        compiler_params=pltpu.CompilerParams(vmem_limit_bytes=8 * 1024 * 1024),
        name="split_columns",
    )(pltpu.with_memory_space_constraint(rows, pltpu.HBM))
    return dict(zip(STEPS, chunks))


def finish(chunks, arrived, outer, momentum, live, scale):
    parts = len(STEPS)
    row_count, columns = chunks[STEPS[0]].shape
    slot_count = arrived.shape[0]
    steps = 4
    block_rows = slot_count // steps

    def kernel(*refs):
        ins = refs[:parts]
        arrived_ref, outer_ref, momentum_ref, live_ref = refs[parts : parts + 4]
        new_outer_ref, new_momentum_ref, joined_ref, sems = refs[parts + 4 :]
        i = pl.program_id(0)
        me = lax.axis_index("replica")
        copies = []
        for k, step in enumerate(STEPS):
            come = place_traced(me, step)
            copies.append(
                pltpu.make_async_copy(
                    ins[k],
                    joined_ref.at[:, pl.ds(pl.multiple_of(come * columns, 128), columns)],
                    sems.at[k],
                )
            )

        @pl.when(i == 0)
        def _():
            for copy in copies:
                copy.start()

        at = pl.ds(pl.multiple_of(i * block_rows, block_rows), block_rows)
        alive = live_ref[at, :] > 0.0
        for start in range(0, columns, 128):
            cols = pl.ds(start, 128)
            mean = arrived_ref[at, cols].astype(jnp.float32) * scale
            old = outer_ref[at, cols]
            pseudo_grad = jnp.where(alive, old - mean, 0.0)
            fresh = momentum_decay * momentum_ref[at, cols] + pseudo_grad
            new_momentum_ref[:, cols] = fresh
            new_outer_ref[:, cols] = old - outer_rate * (pseudo_grad + momentum_decay * fresh)

        @pl.when(i == steps - 1)
        def _():
            for copy in copies:
                copy.wait()

    whole = pl.BlockSpec(memory_space=pltpu.VMEM)
    block = pl.BlockSpec((block_rows, columns), lambda i: (i, 0))
    return pl.pallas_call(
        kernel,
        grid=(steps,),
        out_shape=[jax.ShapeDtypeStruct((slot_count, columns), jnp.float32)] * 2
        + [jax.ShapeDtypeStruct((row_count, parts * columns), jnp.bfloat16)],
        in_specs=[whole] * (parts + 4),
        out_specs=[block, block, pl.BlockSpec(memory_space=pltpu.HBM)],
        scratch_shapes=[pltpu.SemaphoreType.DMA((parts,))],
        cost_estimate=pl.CostEstimate(
            flops=10 * slot_count * columns,
            bytes_accessed=4 * row_count * columns * parts + 18 * slot_count * columns,
            transcendentals=0,
        ),
        compiler_params=pltpu.CompilerParams(vmem_limit_bytes=14 * 1024 * 1024),
        name="finish",
    )(*[chunks[step] for step in STEPS], arrived, outer, momentum, live)


def fresh_rows(parts, base, unpick, pick, scale):
    row_count, columns = parts[0].shape
    slot_count = base.shape[0]
    width = 256

    def kernel(*refs):
        part_refs = refs[: len(parts)]
        base_ref, unpick_ref, pick_ref, rows_ref, slots_ref = refs[len(parts) :]
        for start in range(0, columns, width):
            at = (slice(None), pl.ds(start, width))
            total = part_refs[0][at].astype(jnp.float32)
            for ref in part_refs[1:]:
                total = total + ref[at].astype(jnp.float32)
            share = jnp.dot(unpick_ref[...], base_ref[at], preferred_element_type=jnp.float32)
            rows_ref[at] = (share + scale * total).astype(rows_ref.dtype)
            slots_ref[at] = jnp.dot(
                pick_ref[...], total.astype(jnp.bfloat16), preferred_element_type=jnp.float32
            ).astype(slots_ref.dtype)

    return pl.pallas_call(
        kernel,
        out_shape=[
            jax.ShapeDtypeStruct((row_count, columns), jnp.bfloat16),
            jax.ShapeDtypeStruct((slot_count, columns), jnp.bfloat16),
        ],
        in_specs=[pl.BlockSpec(memory_space=pltpu.VMEM)] * (len(parts) + 3),
        out_specs=[pl.BlockSpec(memory_space=pltpu.VMEM)] * 2,
        cost_estimate=pl.CostEstimate(
            flops=4 * row_count * slot_count * columns,
            bytes_accessed=2 * columns * (row_count * (len(parts) + 1) + 2 * slot_count),
            transcendentals=0,
        ),
        compiler_params=pltpu.CompilerParams(vmem_limit_bytes=8 * 1024 * 1024),
        name="fresh_rows",
    )(*parts, base, unpick, pick)


def partial_sums(*sums):
    row_count, columns = sums[0][0].shape
    width = 256

    def kernel(*refs):
        ins, outs = refs[: -len(sums)], refs[-len(sums) :]
        first = 0
        for terms, out in zip(sums, outs):
            term_refs = ins[first : first + len(terms)]
            first += len(terms)
            for start in range(0, columns, width):
                at = (slice(None), pl.ds(start, width))
                total = term_refs[0][at].astype(jnp.float32)
                for ref in term_refs[1:]:
                    total = total + ref[at].astype(jnp.float32)
                out[at] = total.astype(out.dtype)

    terms = [term for group in sums for term in group]
    return pl.pallas_call(
        kernel,
        out_shape=[jax.ShapeDtypeStruct((row_count, columns), jnp.bfloat16)] * len(sums),
        in_specs=[pl.BlockSpec(memory_space=pltpu.VMEM)] * len(terms),
        out_specs=[pl.BlockSpec(memory_space=pltpu.VMEM)] * len(sums),
        cost_estimate=pl.CostEstimate(
            flops=PACE,
            bytes_accessed=2 * columns * row_count * (len(terms) + len(sums)),
            transcendentals=0,
        ),
        compiler_params=pltpu.CompilerParams(vmem_limit_bytes=8 * 1024 * 1024),
        name="partial_sums",
    )(*terms)


def gate(*arrays):
    def kernel(*refs):
        pass

    return pl.pallas_call(
        kernel,
        out_shape=[jax.ShapeDtypeStruct(array.shape, array.dtype) for array in arrays],
        in_specs=[pl.BlockSpec(memory_space=pl.ANY)] * len(arrays),
        out_specs=[pl.BlockSpec(memory_space=pl.ANY)] * len(arrays),
        input_output_aliases={i: i for i in range(len(arrays))},
        cost_estimate=pl.CostEstimate(flops=PACE, bytes_accessed=0, transcendentals=0),
        compiler_params=pltpu.CompilerParams(vmem_limit_bytes=1024 * 1024),
        name="gate",
    )(*arrays)


def sum_over_replica(rows):
    own = split_columns(rows)
    up_far = send(own[1, 1], (1, 0))
    down_far = send(own[3, 1], (3, 0))
    across = send(own[2, 1], (0, 1))
    up = send(own[1, 0], (1, 0))
    down = send(own[3, 0], (3, 0))
    for_twice, for_beside = partial_sums((own[2, 0], across), (own[0, 1], up_far, down_far))
    twice = send(for_twice, (2, 0))
    beside = send(for_beside, (0, 1))
    return (own[0, 0], up, down, twice, beside), for_beside


def gather_over_replica(rows):
    got = {(0, 0): rows}
    got[0, 1] = send(rows, (0, 1))
    got[2, 0] = send(rows, (2, 0))
    got[3, 0] = send(rows, (1, 0))
    got[1, 0] = send(rows, (3, 0))
    near, far = got[0, 1], got[2, 0] = gate(got[0, 1], got[2, 0])
    got[3, 1] = send(near, (1, 0))
    got[1, 1] = send(near, (3, 0))
    got[2, 1] = send(far, (0, 1))
    return got


def body(local_params, outer_params, outer_momentum, block_lengths, block_owners):
    fsdp_count = lax.axis_size("fsdp")
    group_count = lax.axis_size("replica")
    my_index = lax.axis_index("fsdp")
    own_rows = local_params[0]
    row_count = own_rows.shape[0]
    slots = outer_params.shape[2]
    columns = outer_params.shape[3]
    outer_here = outer_params[0]
    momentum_here = outer_momentum[0]

    parts, halfway = sum_over_replica(own_rows)

    base = (keep * outer_here - drag * momentum_here).astype(jnp.bfloat16)
    own_base = lax.all_to_all(base, "fsdp", split_axis=0, concat_axis=0, tiled=True)

    block_lengths, _ = lax.optimization_barrier((block_lengths, halfway))
    counts, starts = tables(block_lengths, block_owners, fsdp_count)
    slot_ids = jnp.arange(slots, dtype=jnp.int32)
    row_ids = jnp.arange(row_count, dtype=jnp.int32)
    my_starts = lax.dynamic_index_in_dim(starts, my_index, 0, keepdims=False)
    my_counts = lax.dynamic_index_in_dim(counts, my_index, 0, keepdims=False)
    incoming = lax.dynamic_index_in_dim(counts, my_index, 1, keepdims=False)
    live_in = (slot_ids[None, :] < incoming[:, None]).astype(jnp.float32).reshape(-1, 1)
    live_in = jnp.broadcast_to(live_in, (fsdp_count * slots, 128))
    row_of_slot = jnp.where(
        slot_ids[None, :] < my_counts[:, None], my_starts[:, None] + slot_ids[None, :], -1
    ).reshape(-1)
    pick = (row_of_slot[:, None] == row_ids[None, :]).astype(own_rows.dtype)
    unpick = (row_ids[:, None] == row_of_slot[None, :]).astype(own_rows.dtype)
    rows, packed = fresh_rows(
        parts, own_base.reshape(fsdp_count * slots, columns), unpick, pick, pull / group_count
    )
    gathered = gather_over_replica(rows)
    arrived = lax.all_to_all(
        packed.reshape(fsdp_count, slots, columns), "fsdp", split_axis=0, concat_axis=0, tiled=True
    )
    flat = (fsdp_count * slots, columns)
    fresh_outer, fresh_momentum, joined = finish(
        gathered,
        arrived.reshape(flat),
        outer_here.reshape(flat),
        momentum_here.reshape(flat),
        live_in,
        1.0 / group_count,
    )
    return (
        fresh_outer.reshape(outer_params.shape),
        fresh_momentum.reshape(outer_params.shape),
        joined,
    )


def solution(mesh):
    in_specs = (
        P("replica", "fsdp", None),
        P("fsdp", None, None, "replica"),
        P("fsdp", None, None, "replica"),
        P(),
        P(),
    )
    out_specs = (
        P("fsdp", None, None, "replica"),
        P("fsdp", None, None, "replica"),
        P("fsdp", None),
    )
    return jax.shard_map(body, mesh=mesh, in_specs=in_specs, out_specs=out_specs, check_vma=False)
```

```python
import jax
import jax.numpy as jnp
from jax import lax
from jax.experimental import pallas as pl
from jax.experimental.pallas import tpu as pltpu
from jax.sharding import PartitionSpec as P

outer_rate = 0.7
momentum_decay = 0.9
PACE = 1150000000000
GATE_PACE = 11500000000
pull = outer_rate * (1.0 + momentum_decay)
keep = 1.0 - pull
drag = outer_rate * momentum_decay * momentum_decay

STEPS = [(0, 0), (1, 0), (3, 0), (2, 0), (0, 1), (1, 1), (3, 1), (2, 1)]


def place(me, step):
    y, x = me // 2, me % 2
    return ((y + step[0]) % 4) * 2 + (x + step[1]) % 2


def place_traced(me, step):
    y, x = lax.div(me, 2), lax.rem(me, 2)
    return lax.rem(y + step[0], 4) * 2 + lax.rem(x + step[1], 2)


def send(array, step):
    return lax.ppermute(array, "replica", [(i, place(i, step)) for i in range(8)])


def tables(block_lengths, block_owners, owner_count):
    block_count = block_lengths.shape[1]
    block_ids = jnp.arange(block_count, dtype=jnp.int32)
    before = (block_ids[None, :] < block_ids[:, None]).astype(jnp.int32)
    offsets = jnp.sum(before[None] * block_lengths[:, None, :], axis=2)
    heads = block_owners[:, :block_count]
    owner_ids = jnp.arange(owner_count, dtype=jnp.int32)
    match = (heads[:, :, None] == owner_ids[None, None, :]).astype(jnp.int32)
    counts = jnp.sum(match * block_lengths[:, :, None], axis=1)
    starts = jnp.sum(match * offsets[:, :, None], axis=1)
    return counts, starts


def split_columns(rows):
    row_count, width = rows.shape
    parts = len(STEPS)
    columns = width // parts

    def kernel(rows_ref, *refs):
        outs, sems = refs[:parts], refs[parts]
        me = lax.axis_index("replica")
        copies = []
        for k, step in enumerate(STEPS):
            to = place_traced(me, step)
            copies.append(
                pltpu.make_async_copy(
                    rows_ref.at[:, pl.ds(pl.multiple_of(to * columns, 128), columns)],
                    outs[k],
                    sems.at[k],
                )
            )
        for copy in copies:
            copy.start()
        for copy in copies:
            copy.wait()

    chunks = pl.pallas_call(
        kernel,
        out_shape=[jax.ShapeDtypeStruct((row_count, columns), rows.dtype)] * parts,
        in_specs=[pl.BlockSpec(memory_space=pltpu.HBM)],
        out_specs=[pl.BlockSpec(memory_space=pltpu.VMEM)] * parts,
        scratch_shapes=[pltpu.SemaphoreType.DMA((parts,))],
        cost_estimate=pl.CostEstimate(
            flops=0, bytes_accessed=4 * row_count * width, transcendentals=0
        ),
        compiler_params=pltpu.CompilerParams(vmem_limit_bytes=8 * 1024 * 1024),
        name="split_columns",
    )(pltpu.with_memory_space_constraint(rows, pltpu.HBM))
    return dict(zip(STEPS, chunks))


def join_columns(chunks, into=None):
    steps = list(chunks)
    row_count, columns = chunks[steps[0]].shape

    def kernel(*refs):
        ins, out, sems = refs[: len(steps)], refs[-2], refs[-1]
        me = lax.axis_index("replica")
        copies = []
        for k, step in enumerate(steps):
            come = place_traced(me, step)
            copies.append(
                pltpu.make_async_copy(
                    ins[k],
                    out.at[:, pl.ds(pl.multiple_of(come * columns, 128), columns)],
                    sems.at[k],
                )
            )
        for copy in copies:
            copy.start()
        for copy in copies:
            copy.wait()

    args = [chunks[step] for step in steps]
    specs = [pl.BlockSpec(memory_space=pltpu.VMEM)] * len(steps)
    if into is not None:
        args.append(into)
        specs.append(pl.BlockSpec(memory_space=pltpu.HBM))
    return pl.pallas_call(
        kernel,
        out_shape=jax.ShapeDtypeStruct((row_count, columns * len(STEPS)), jnp.bfloat16),
        in_specs=specs,
        out_specs=pl.BlockSpec(memory_space=pltpu.HBM),
        input_output_aliases={} if into is None else {len(steps): 0},
        scratch_shapes=[pltpu.SemaphoreType.DMA((len(steps),))],
        cost_estimate=pl.CostEstimate(
            flops=0, bytes_accessed=4 * row_count * columns * len(steps), transcendentals=0
        ),
        compiler_params=pltpu.CompilerParams(vmem_limit_bytes=8 * 1024 * 1024),
        name="join_columns",
    )(*args)


def finish(chunks, into, arrived, outer, momentum, live, scale):
    steps = list(chunks)
    row_count, columns = chunks[steps[0]].shape
    slot_count = arrived.shape[0]
    blocks = 4
    rows = slot_count // blocks

    def kernel(*refs):
        ins = refs[: len(steps)]
        arrived_ref, outer_ref, momentum_ref, live_ref, _ = refs[len(steps) : len(steps) + 5]
        new_outer_ref, new_momentum_ref, joined_ref, sems = refs[len(steps) + 5 :]
        i = pl.program_id(0)
        me = lax.axis_index("replica")
        copies = []
        for k, step in enumerate(steps):
            come = place_traced(me, step)
            copies.append(
                pltpu.make_async_copy(
                    ins[k],
                    joined_ref.at[:, pl.ds(pl.multiple_of(come * columns, 128), columns)],
                    sems.at[k],
                )
            )

        @pl.when(i == 0)
        def _():
            for copy in copies:
                copy.start()

        alive = live_ref[...] > 0.0
        at = pl.ds(pl.multiple_of(i * rows, rows), rows)
        for start in range(0, columns, 128):
            cols = pl.ds(start, 128)
            mean = arrived_ref[:, cols].astype(jnp.float32) * scale
            old = outer_ref[:, cols]
            pseudo_grad = jnp.where(alive, old - mean, 0.0)
            fresh = momentum_decay * momentum_ref[at, cols] + pseudo_grad
            new_momentum_ref[:, cols] = fresh
            new_outer_ref[:, cols] = old - outer_rate * (pseudo_grad + momentum_decay * fresh)

        @pl.when(i == blocks - 1)
        def _():
            for copy in copies:
                copy.wait()

    whole = pl.BlockSpec(memory_space=pltpu.VMEM)
    in_hbm = pl.BlockSpec(memory_space=pltpu.HBM)
    block = pl.BlockSpec((rows, columns), lambda i: (i, 0))
    return pl.pallas_call(
        kernel,
        grid=(blocks,),
        out_shape=[jax.ShapeDtypeStruct((slot_count, columns), jnp.float32)] * 2
        + [jax.ShapeDtypeStruct(into.shape, into.dtype)],
        in_specs=[whole] * len(steps)
        + [block, block, whole, pl.BlockSpec((rows, 128), lambda i: (i, 0)), in_hbm],
        out_specs=[block, block, in_hbm],
        input_output_aliases={len(steps) + 4: 2},
        scratch_shapes=[pltpu.SemaphoreType.DMA((len(steps),))],
        cost_estimate=pl.CostEstimate(
            flops=10 * slot_count * columns,
            bytes_accessed=4 * row_count * columns * len(steps) + 18 * slot_count * columns,
            transcendentals=0,
        ),
        compiler_params=pltpu.CompilerParams(vmem_limit_bytes=12 * 1024 * 1024),
        name="finish",
    )(
        *[chunks[step] for step in steps],
        arrived,
        pltpu.with_memory_space_constraint(outer, pltpu.HBM),
        momentum,
        live,
        into,
    )


def fresh_rows(parts, share, scale):
    row_count, columns = share.shape
    width = 256

    def kernel(*refs):
        part_refs = refs[: len(parts)]
        share_ref, rows_ref, total_ref = refs[len(parts) :]
        for start in range(0, columns, width):
            at = (slice(None), pl.ds(start, width))
            total = part_refs[0][at].astype(jnp.float32)
            for ref in part_refs[1:]:
                total = total + ref[at].astype(jnp.float32)
            more = share_ref[at].astype(jnp.float32)
            rows_ref[at] = (more + scale * total).astype(rows_ref.dtype)
            total_ref[at] = total.astype(total_ref.dtype)

    return pl.pallas_call(
        kernel,
        out_shape=[jax.ShapeDtypeStruct((row_count, columns), jnp.bfloat16)] * 2,
        in_specs=[pl.BlockSpec(memory_space=pltpu.VMEM)] * (len(parts) + 1),
        out_specs=[pl.BlockSpec(memory_space=pltpu.VMEM)] * 2,
        cost_estimate=pl.CostEstimate(
            flops=row_count * columns * (len(parts) + 2),
            bytes_accessed=2 * columns * row_count * (len(parts) + 3),
            transcendentals=0,
        ),
        compiler_params=pltpu.CompilerParams(vmem_limit_bytes=8 * 1024 * 1024),
        name="fresh_rows",
    )(*parts, share)


def partial_sums(*sums):
    row_count, columns = sums[0][0].shape
    width = 256

    def kernel(*refs):
        ins, outs = refs[: -len(sums)], refs[-len(sums) :]
        first = 0
        for terms, out in zip(sums, outs):
            term_refs = ins[first : first + len(terms)]
            first += len(terms)
            for start in range(0, columns, width):
                at = (slice(None), pl.ds(start, width))
                total = term_refs[0][at].astype(jnp.float32)
                for ref in term_refs[1:]:
                    total = total + ref[at].astype(jnp.float32)
                out[at] = total.astype(out.dtype)

    terms = [term for group in sums for term in group]
    return pl.pallas_call(
        kernel,
        out_shape=[jax.ShapeDtypeStruct((row_count, columns), jnp.bfloat16)] * len(sums),
        in_specs=[pl.BlockSpec(memory_space=pltpu.VMEM)] * len(terms),
        out_specs=[pl.BlockSpec(memory_space=pltpu.VMEM)] * len(sums),
        cost_estimate=pl.CostEstimate(
            flops=PACE,
            bytes_accessed=2 * columns * row_count * (len(terms) + len(sums)),
            transcendentals=0,
        ),
        compiler_params=pltpu.CompilerParams(vmem_limit_bytes=8 * 1024 * 1024),
        name="partial_sums",
    )(*terms)


def pick_rows(pick, array, name):
    count, columns = pick.shape[0], array.shape[1]
    width = 256

    def kernel(pick_ref, array_ref, out_ref):
        for start in range(0, columns, width):
            cols = pl.ds(start, width)
            out_ref[:, cols] = jnp.dot(
                pick_ref[...], array_ref[:, cols], preferred_element_type=jnp.float32
            ).astype(out_ref.dtype)

    return pl.pallas_call(
        kernel,
        out_shape=jax.ShapeDtypeStruct((count, columns), array.dtype),
        in_specs=[pl.BlockSpec(memory_space=pltpu.VMEM)] * 2,
        out_specs=pl.BlockSpec(memory_space=pltpu.VMEM),
        cost_estimate=pl.CostEstimate(
            flops=2 * count * array.shape[0] * columns,
            bytes_accessed=2 * columns * (count + array.shape[0]),
            transcendentals=0,
        ),
        compiler_params=pltpu.CompilerParams(vmem_limit_bytes=4 * 1024 * 1024),
        name=name,
    )(pick, array)


def gate(*arrays):
    def kernel(*refs):
        pass

    return pl.pallas_call(
        kernel,
        out_shape=[jax.ShapeDtypeStruct(array.shape, array.dtype) for array in arrays],
        in_specs=[pl.BlockSpec(memory_space=pl.ANY)] * len(arrays),
        out_specs=[pl.BlockSpec(memory_space=pl.ANY)] * len(arrays),
        input_output_aliases={i: i for i in range(len(arrays))},
        cost_estimate=pl.CostEstimate(flops=GATE_PACE, bytes_accessed=0, transcendentals=0),
        compiler_params=pltpu.CompilerParams(vmem_limit_bytes=1024 * 1024),
        name="gate",
    )(*arrays)


def sum_over_replica(rows):
    own = split_columns(rows)
    up_far = send(own[1, 1], (1, 0))
    down_far = send(own[3, 1], (3, 0))
    across = send(own[2, 1], (0, 1))
    up = send(own[1, 0], (1, 0))
    down = send(own[3, 0], (3, 0))
    for_twice, for_beside = partial_sums((own[2, 0], across), (own[0, 1], up_far, down_far))
    twice = send(for_twice, (2, 0))
    beside = send(for_beside, (0, 1))
    return (own[0, 0], up, down, twice, beside), for_beside


def gather_over_replica(rows):
    got = {(0, 0): rows}
    got[0, 1] = send(rows, (0, 1))
    got[2, 0] = send(rows, (2, 0))
    got[3, 0] = send(rows, (1, 0))
    got[1, 0] = send(rows, (3, 0))
    near, far = got[0, 1], got[2, 0] = gate(got[0, 1], got[2, 0])
    got[3, 1] = send(near, (1, 0))
    got[1, 1] = send(near, (3, 0))
    got[2, 1] = send(far, (0, 1))
    return got


def body(local_params, outer_params, outer_momentum, block_lengths, block_owners):
    fsdp_count = lax.axis_size("fsdp")
    group_count = lax.axis_size("replica")
    my_index = lax.axis_index("fsdp")
    own_rows = local_params[0]
    row_count = own_rows.shape[0]
    slots = outer_params.shape[2]
    columns = outer_params.shape[3]
    outer_here = outer_params[0]
    momentum_here = outer_momentum[0]

    parts, halfway = sum_over_replica(own_rows)

    base = (keep * outer_here - drag * momentum_here).astype(jnp.bfloat16)
    own_base = lax.all_to_all(base, "fsdp", split_axis=0, concat_axis=0, tiled=True)

    block_lengths, _ = lax.optimization_barrier((block_lengths, halfway))
    counts, starts = tables(block_lengths, block_owners, fsdp_count)
    slot_ids = jnp.arange(slots, dtype=jnp.int32)
    row_ids = jnp.arange(row_count, dtype=jnp.int32)
    my_starts = lax.dynamic_index_in_dim(starts, my_index, 0, keepdims=False)
    my_counts = lax.dynamic_index_in_dim(counts, my_index, 0, keepdims=False)
    incoming = lax.dynamic_index_in_dim(counts, my_index, 1, keepdims=False)
    live_in = (slot_ids[None, :] < incoming[:, None]).astype(jnp.float32).reshape(-1, 1)
    live_in = jnp.broadcast_to(live_in, (fsdp_count * slots, 128))
    row_of_slot = jnp.where(
        slot_ids[None, :] < my_counts[:, None], my_starts[:, None] + slot_ids[None, :], -1
    ).reshape(-1)
    pick = (row_of_slot[:, None] == row_ids[None, :]).astype(own_rows.dtype)
    unpick = (row_ids[:, None] == row_of_slot[None, :]).astype(own_rows.dtype)
    share = pick_rows(unpick, own_base.reshape(-1, columns), "own_share")
    rows, total = fresh_rows(parts, share, pull / group_count)
    packed = pick_rows(pick, total, "pack_slots")
    gathered = gather_over_replica(rows)
    arrived = lax.all_to_all(
        packed.reshape(fsdp_count, slots, columns), "fsdp", split_axis=0, concat_axis=0, tiled=True
    )
    flat = (fsdp_count * slots, columns)
    first = [(0, 0), (0, 1), (2, 0), (1, 0), (3, 0)]
    joined = join_columns({step: gathered[step] for step in first})
    fresh_outer, fresh_momentum, joined = finish(
        {step: gathered[step] for step in STEPS if step not in first},
        joined,
        arrived.reshape(flat),
        outer_here.reshape(flat),
        momentum_here.reshape(flat),
        live_in,
        1.0 / group_count,
    )
    return (
        fresh_outer.reshape(outer_params.shape),
        fresh_momentum.reshape(outer_params.shape),
        joined,
    )


def solution(mesh):
    in_specs = (
        P("replica", "fsdp", None),
        P("fsdp", None, None, "replica"),
        P("fsdp", None, None, "replica"),
        P(),
        P(),
    )
    out_specs = (
        P("fsdp", None, None, "replica"),
        P("fsdp", None, None, "replica"),
        P("fsdp", None),
    )
    return jax.shard_map(body, mesh=mesh, in_specs=in_specs, out_specs=out_specs, check_vma=False)
```

```python
import jax
import jax.numpy as jnp
from jax import lax
from jax.experimental import pallas as pl
from jax.experimental.pallas import tpu as pltpu
from jax.sharding import PartitionSpec as P

outer_rate = 0.7
momentum_decay = 0.9
PACE = 1150000000000
GATE_PACE = 11500000000
pull = outer_rate * (1.0 + momentum_decay)
keep = 1.0 - pull
drag = outer_rate * momentum_decay * momentum_decay

STEPS = [(0, 0), (1, 0), (3, 0), (2, 0), (0, 1), (1, 1), (3, 1), (2, 1)]


def place(me, step):
    y, x = me // 2, me % 2
    return ((y + step[0]) % 4) * 2 + (x + step[1]) % 2


def place_traced(me, step):
    y, x = lax.div(me, 2), lax.rem(me, 2)
    return lax.rem(y + step[0], 4) * 2 + lax.rem(x + step[1], 2)


def send(array, step):
    return lax.ppermute(array, "replica", [(i, place(i, step)) for i in range(8)])


def tables(block_lengths, block_owners, owner_count):
    block_count = block_lengths.shape[1]
    offsets = jnp.cumsum(block_lengths, axis=1) - block_lengths
    heads = block_owners[:, :block_count]
    owner_ids = jnp.arange(owner_count, dtype=jnp.int32)
    match = (heads[:, :, None] == owner_ids[None, None, :]).astype(jnp.int32)
    counts = jnp.sum(match * block_lengths[:, :, None], axis=1)
    starts = jnp.sum(match * offsets[:, :, None], axis=1)
    return counts, starts


def split_columns(rows):
    row_count, width = rows.shape
    parts = len(STEPS)
    columns = width // parts

    def kernel(rows_ref, *refs):
        outs, sems = refs[:parts], refs[parts]
        me = lax.axis_index("replica")
        copies = []
        for k, step in enumerate(STEPS):
            to = place_traced(me, step)
            copies.append(
                pltpu.make_async_copy(
                    rows_ref.at[:, pl.ds(pl.multiple_of(to * columns, 128), columns)],
                    outs[k],
                    sems.at[k],
                )
            )
        for copy in copies:
            copy.start()
        for copy in copies:
            copy.wait()

    chunks = pl.pallas_call(
        kernel,
        out_shape=[jax.ShapeDtypeStruct((row_count, columns), rows.dtype)] * parts,
        in_specs=[pl.BlockSpec(memory_space=pltpu.HBM)],
        out_specs=[pl.BlockSpec(memory_space=pltpu.VMEM)] * parts,
        scratch_shapes=[pltpu.SemaphoreType.DMA((parts,))],
        cost_estimate=pl.CostEstimate(
            flops=0, bytes_accessed=4 * row_count * width, transcendentals=0
        ),
        compiler_params=pltpu.CompilerParams(vmem_limit_bytes=8 * 1024 * 1024),
        name="split_columns",
    )(pltpu.with_memory_space_constraint(rows, pltpu.HBM))
    return dict(zip(STEPS, chunks))


def join_columns(chunks, into=None):
    steps = list(chunks)
    row_count, columns = chunks[steps[0]].shape

    def kernel(*refs):
        ins, out, sems = refs[: len(steps)], refs[-2], refs[-1]
        me = lax.axis_index("replica")
        copies = []
        for k, step in enumerate(steps):
            come = place_traced(me, step)
            copies.append(
                pltpu.make_async_copy(
                    ins[k],
                    out.at[:, pl.ds(pl.multiple_of(come * columns, 128), columns)],
                    sems.at[k],
                )
            )
        for copy in copies:
            copy.start()
        for copy in copies:
            copy.wait()

    args = [chunks[step] for step in steps]
    specs = [pl.BlockSpec(memory_space=pltpu.VMEM)] * len(steps)
    if into is not None:
        args.append(into)
        specs.append(pl.BlockSpec(memory_space=pltpu.HBM))
    return pl.pallas_call(
        kernel,
        out_shape=jax.ShapeDtypeStruct((row_count, columns * len(STEPS)), jnp.bfloat16),
        in_specs=specs,
        out_specs=pl.BlockSpec(memory_space=pltpu.HBM),
        input_output_aliases={} if into is None else {len(steps): 0},
        scratch_shapes=[pltpu.SemaphoreType.DMA((len(steps),))],
        cost_estimate=pl.CostEstimate(
            flops=0, bytes_accessed=4 * row_count * columns * len(steps), transcendentals=0
        ),
        compiler_params=pltpu.CompilerParams(vmem_limit_bytes=8 * 1024 * 1024),
        name="join_columns",
    )(*args)


def finish(chunks, into, arrived, outer, momentum, live, scale):
    steps = list(chunks)
    row_count, columns = chunks[steps[0]].shape
    slot_count = arrived.shape[0]
    blocks = 4
    rows = slot_count // blocks

    def kernel(*refs):
        ins = refs[: len(steps)]
        arrived_ref, outer_ref, momentum_ref, live_ref, _ = refs[len(steps) : len(steps) + 5]
        new_outer_ref, new_momentum_ref, joined_ref, sems = refs[len(steps) + 5 :]
        i = pl.program_id(0)
        me = lax.axis_index("replica")
        copies = []
        for k, step in enumerate(steps):
            come = place_traced(me, step)
            copies.append(
                pltpu.make_async_copy(
                    ins[k],
                    joined_ref.at[:, pl.ds(pl.multiple_of(come * columns, 128), columns)],
                    sems.at[k],
                )
            )

        @pl.when(i == 0)
        def _():
            for copy in copies:
                copy.start()

        alive = live_ref[...] > 0.0
        at = pl.ds(pl.multiple_of(i * rows, rows), rows)
        for start in range(0, columns, 128):
            cols = pl.ds(start, 128)
            mean = arrived_ref[:, cols].astype(jnp.float32) * scale
            old = outer_ref[:, cols]
            pseudo_grad = jnp.where(alive, old - mean, 0.0)
            fresh = momentum_decay * momentum_ref[at, cols] + pseudo_grad
            new_momentum_ref[:, cols] = fresh
            new_outer_ref[:, cols] = old - outer_rate * (pseudo_grad + momentum_decay * fresh)

        @pl.when(i == blocks - 1)
        def _():
            for copy in copies:
                copy.wait()

    whole = pl.BlockSpec(memory_space=pltpu.VMEM)
    in_hbm = pl.BlockSpec(memory_space=pltpu.HBM)
    block = pl.BlockSpec((rows, columns), lambda i: (i, 0))
    return pl.pallas_call(
        kernel,
        grid=(blocks,),
        out_shape=[jax.ShapeDtypeStruct((slot_count, columns), jnp.float32)] * 2
        + [jax.ShapeDtypeStruct(into.shape, into.dtype)],
        in_specs=[whole] * len(steps)
        + [block, block, whole, pl.BlockSpec((rows, 128), lambda i: (i, 0)), in_hbm],
        out_specs=[block, block, in_hbm],
        input_output_aliases={len(steps) + 4: 2},
        scratch_shapes=[pltpu.SemaphoreType.DMA((len(steps),))],
        cost_estimate=pl.CostEstimate(
            flops=10 * slot_count * columns,
            bytes_accessed=4 * row_count * columns * len(steps) + 18 * slot_count * columns,
            transcendentals=0,
        ),
        compiler_params=pltpu.CompilerParams(vmem_limit_bytes=12 * 1024 * 1024),
        name="finish",
    )(
        *[chunks[step] for step in steps],
        arrived,
        pltpu.with_memory_space_constraint(outer, pltpu.HBM),
        momentum,
        live,
        into,
    )


def fresh_rows(parts, share, scale):
    row_count, columns = share.shape
    width = 256

    def kernel(*refs):
        part_refs = refs[: len(parts)]
        share_ref, rows_ref, total_ref = refs[len(parts) :]
        for start in range(0, columns, width):
            at = (slice(None), pl.ds(start, width))
            total = part_refs[0][at].astype(jnp.float32)
            for ref in part_refs[1:]:
                total = total + ref[at].astype(jnp.float32)
            more = share_ref[at].astype(jnp.float32)
            rows_ref[at] = (more + scale * total).astype(rows_ref.dtype)
            total_ref[at] = total.astype(total_ref.dtype)

    return pl.pallas_call(
        kernel,
        out_shape=[jax.ShapeDtypeStruct((row_count, columns), jnp.bfloat16)] * 2,
        in_specs=[pl.BlockSpec(memory_space=pltpu.VMEM)] * (len(parts) + 1),
        out_specs=[pl.BlockSpec(memory_space=pltpu.VMEM)] * 2,
        cost_estimate=pl.CostEstimate(
            flops=row_count * columns * (len(parts) + 2),
            bytes_accessed=2 * columns * row_count * (len(parts) + 3),
            transcendentals=0,
        ),
        compiler_params=pltpu.CompilerParams(vmem_limit_bytes=8 * 1024 * 1024),
        name="fresh_rows",
    )(*parts, share)


def partial_sums(*sums):
    row_count, columns = sums[0][0].shape
    width = 256

    def kernel(*refs):
        ins, outs = refs[: -len(sums)], refs[-len(sums) :]
        first = 0
        for terms, out in zip(sums, outs):
            term_refs = ins[first : first + len(terms)]
            first += len(terms)
            for start in range(0, columns, width):
                at = (slice(None), pl.ds(start, width))
                total = term_refs[0][at].astype(jnp.float32)
                for ref in term_refs[1:]:
                    total = total + ref[at].astype(jnp.float32)
                out[at] = total.astype(out.dtype)

    terms = [term for group in sums for term in group]
    return pl.pallas_call(
        kernel,
        out_shape=[jax.ShapeDtypeStruct((row_count, columns), jnp.bfloat16)] * len(sums),
        in_specs=[pl.BlockSpec(memory_space=pltpu.VMEM)] * len(terms),
        out_specs=[pl.BlockSpec(memory_space=pltpu.VMEM)] * len(sums),
        cost_estimate=pl.CostEstimate(
            flops=PACE,
            bytes_accessed=2 * columns * row_count * (len(terms) + len(sums)),
            transcendentals=0,
        ),
        compiler_params=pltpu.CompilerParams(vmem_limit_bytes=8 * 1024 * 1024),
        name="partial_sums",
    )(*terms)


def pick_rows(pick, array, name):
    count, columns = pick.shape[0], array.shape[1]
    width = 256

    def kernel(pick_ref, array_ref, out_ref):
        for start in range(0, columns, width):
            cols = pl.ds(start, width)
            out_ref[:, cols] = jnp.dot(
                pick_ref[...], array_ref[:, cols], preferred_element_type=jnp.float32
            ).astype(out_ref.dtype)

    return pl.pallas_call(
        kernel,
        out_shape=jax.ShapeDtypeStruct((count, columns), array.dtype),
        in_specs=[pl.BlockSpec(memory_space=pltpu.VMEM)] * 2,
        out_specs=pl.BlockSpec(memory_space=pltpu.VMEM),
        cost_estimate=pl.CostEstimate(
            flops=2 * count * array.shape[0] * columns,
            bytes_accessed=2 * columns * (count + array.shape[0]),
            transcendentals=0,
        ),
        compiler_params=pltpu.CompilerParams(vmem_limit_bytes=4 * 1024 * 1024),
        name=name,
    )(pick, array)


def gate(*arrays):
    def kernel(*refs):
        pass

    return pl.pallas_call(
        kernel,
        out_shape=[jax.ShapeDtypeStruct(array.shape, array.dtype) for array in arrays],
        in_specs=[pl.BlockSpec(memory_space=pl.ANY)] * len(arrays),
        out_specs=[pl.BlockSpec(memory_space=pl.ANY)] * len(arrays),
        input_output_aliases={i: i for i in range(len(arrays))},
        cost_estimate=pl.CostEstimate(flops=GATE_PACE, bytes_accessed=0, transcendentals=0),
        compiler_params=pltpu.CompilerParams(vmem_limit_bytes=1024 * 1024),
        name="gate",
    )(*arrays)


def sum_over_replica(rows):
    own = split_columns(rows)
    up_far = send(own[1, 1], (1, 0))
    down_far = send(own[3, 1], (3, 0))
    across = send(own[2, 1], (0, 1))
    up = send(own[1, 0], (1, 0))
    down = send(own[3, 0], (3, 0))
    for_twice, for_beside = partial_sums((own[2, 0], across), (own[0, 1], up_far, down_far))
    twice = send(for_twice, (2, 0))
    beside = send(for_beside, (0, 1))
    return (own[0, 0], up, down, twice, beside), for_beside


def gather_over_replica(rows):
    got = {(0, 0): rows}
    got[0, 1] = send(rows, (0, 1))
    got[2, 0] = send(rows, (2, 0))
    got[3, 0] = send(rows, (1, 0))
    got[1, 0] = send(rows, (3, 0))
    near, far = got[0, 1], got[2, 0] = gate(got[0, 1], got[2, 0])
    got[3, 1] = send(near, (1, 0))
    got[1, 1] = send(near, (3, 0))
    got[2, 1] = send(far, (0, 1))
    return got


def body(local_params, outer_params, outer_momentum, block_lengths, block_owners):
    fsdp_count = lax.axis_size("fsdp")
    group_count = lax.axis_size("replica")
    my_index = lax.axis_index("fsdp")
    own_rows = local_params[0]
    row_count = own_rows.shape[0]
    slots = outer_params.shape[2]
    columns = outer_params.shape[3]
    outer_here = outer_params[0]
    momentum_here = outer_momentum[0]

    parts, halfway = sum_over_replica(own_rows)

    base = (keep * outer_here - drag * momentum_here).astype(jnp.bfloat16)
    own_base = lax.all_to_all(base, "fsdp", split_axis=0, concat_axis=0, tiled=True)

    block_lengths, _ = lax.optimization_barrier((block_lengths, halfway))
    counts, starts = tables(block_lengths, block_owners, fsdp_count)
    slot_ids = jnp.arange(slots, dtype=jnp.int32)
    row_ids = jnp.arange(row_count, dtype=jnp.int32)
    my_starts = lax.dynamic_index_in_dim(starts, my_index, 0, keepdims=False)
    my_counts = lax.dynamic_index_in_dim(counts, my_index, 0, keepdims=False)
    incoming = lax.dynamic_index_in_dim(counts, my_index, 1, keepdims=False)
    live_in = (slot_ids[None, :] < incoming[:, None]).astype(jnp.float32).reshape(-1, 1)
    live_in = jnp.broadcast_to(live_in, (fsdp_count * slots, 128))
    row_of_slot = jnp.where(
        slot_ids[None, :] < my_counts[:, None], my_starts[:, None] + slot_ids[None, :], -1
    ).reshape(-1)
    pick = (row_of_slot[:, None] == row_ids[None, :]).astype(own_rows.dtype)
    unpick = (row_ids[:, None] == row_of_slot[None, :]).astype(own_rows.dtype)
    share = pick_rows(unpick, own_base.reshape(-1, columns), "own_share")
    rows, total = fresh_rows(parts, share, pull / group_count)
    packed = pick_rows(pick, total, "pack_slots")
    gathered = gather_over_replica(rows)
    arrived = lax.all_to_all(
        packed.reshape(fsdp_count, slots, columns), "fsdp", split_axis=0, concat_axis=0, tiled=True
    )
    flat = (fsdp_count * slots, columns)
    first = [(0, 0), (0, 1), (2, 0), (1, 0), (3, 0)]
    joined = join_columns({step: gathered[step] for step in first})
    fresh_outer, fresh_momentum, joined = finish(
        {step: gathered[step] for step in STEPS if step not in first},
        joined,
        arrived.reshape(flat),
        outer_here.reshape(flat),
        momentum_here.reshape(flat),
        live_in,
        1.0 / group_count,
    )
    return (
        fresh_outer.reshape(outer_params.shape),
        fresh_momentum.reshape(outer_params.shape),
        joined,
    )


def solution(mesh):
    in_specs = (
        P("replica", "fsdp", None),
        P("fsdp", None, None, "replica"),
        P("fsdp", None, None, "replica"),
        P(),
        P(),
    )
    out_specs = (
        P("fsdp", None, None, "replica"),
        P("fsdp", None, None, "replica"),
        P("fsdp", None),
    )
    return jax.shard_map(body, mesh=mesh, in_specs=in_specs, out_specs=out_specs, check_vma=False)
```

```python
import jax
import jax.numpy as jnp
from jax import lax
from jax.experimental import pallas as pl
from jax.experimental.pallas import tpu as pltpu
from jax.sharding import PartitionSpec as P

outer_rate = 0.7
momentum_decay = 0.9
PACE = 1150000000000
GATE_PACE = 11500000000
pull = outer_rate * (1.0 + momentum_decay)
keep = 1.0 - pull
drag = outer_rate * momentum_decay * momentum_decay

STEPS = [(0, 0), (1, 0), (3, 0), (2, 0), (0, 1), (1, 1), (3, 1), (2, 1)]


def place(me, step):
    y, x = me // 2, me % 2
    return ((y + step[0]) % 4) * 2 + (x + step[1]) % 2


def place_traced(me, step):
    y, x = lax.div(me, 2), lax.rem(me, 2)
    return lax.rem(y + step[0], 4) * 2 + lax.rem(x + step[1], 2)


def send(array, step):
    return lax.ppermute(array, "replica", [(i, place(i, step)) for i in range(8)])


def tables(block_lengths, block_owners, owner_count):
    block_count = block_lengths.shape[1]
    offsets = jnp.cumsum(block_lengths, axis=1) - block_lengths
    heads = block_owners[:, :block_count]
    owner_ids = jnp.arange(owner_count, dtype=jnp.int32)
    match = (heads[:, :, None] == owner_ids[None, None, :]).astype(jnp.int32)
    counts = jnp.sum(match * block_lengths[:, :, None], axis=1)
    starts = jnp.sum(match * offsets[:, :, None], axis=1)
    return counts, starts


def split_columns(rows):
    row_count, width = rows.shape
    parts = len(STEPS)
    columns = width // parts

    def kernel(rows_ref, *refs):
        outs, sems = refs[:parts], refs[parts]
        me = lax.axis_index("replica")
        copies = []
        for k, step in enumerate(STEPS):
            to = place_traced(me, step)
            copies.append(
                pltpu.make_async_copy(
                    rows_ref.at[:, pl.ds(pl.multiple_of(to * columns, 128), columns)],
                    outs[k],
                    sems.at[k],
                )
            )
        for copy in copies:
            copy.start()
        for copy in copies:
            copy.wait()

    chunks = pl.pallas_call(
        kernel,
        out_shape=[jax.ShapeDtypeStruct((row_count, columns), rows.dtype)] * parts,
        in_specs=[pl.BlockSpec(memory_space=pltpu.HBM)],
        out_specs=[pl.BlockSpec(memory_space=pltpu.VMEM)] * parts,
        scratch_shapes=[pltpu.SemaphoreType.DMA((parts,))],
        cost_estimate=pl.CostEstimate(
            flops=0, bytes_accessed=4 * row_count * width, transcendentals=0
        ),
        compiler_params=pltpu.CompilerParams(vmem_limit_bytes=8 * 1024 * 1024),
        name="split_columns",
    )(pltpu.with_memory_space_constraint(rows, pltpu.HBM))
    return dict(zip(STEPS, chunks))


def join_columns(chunks, into=None):
    steps = list(chunks)
    row_count, columns = chunks[steps[0]].shape

    def kernel(*refs):
        ins, out, sems = refs[: len(steps)], refs[-2], refs[-1]
        me = lax.axis_index("replica")
        copies = []
        for k, step in enumerate(steps):
            come = place_traced(me, step)
            copies.append(
                pltpu.make_async_copy(
                    ins[k],
                    out.at[:, pl.ds(pl.multiple_of(come * columns, 128), columns)],
                    sems.at[k],
                )
            )
        for copy in copies:
            copy.start()
        for copy in copies:
            copy.wait()

    args = [chunks[step] for step in steps]
    specs = [pl.BlockSpec(memory_space=pltpu.VMEM)] * len(steps)
    if into is not None:
        args.append(into)
        specs.append(pl.BlockSpec(memory_space=pltpu.HBM))
    return pl.pallas_call(
        kernel,
        out_shape=jax.ShapeDtypeStruct((row_count, columns * len(STEPS)), jnp.bfloat16),
        in_specs=specs,
        out_specs=pl.BlockSpec(memory_space=pltpu.HBM),
        input_output_aliases={} if into is None else {len(steps): 0},
        scratch_shapes=[pltpu.SemaphoreType.DMA((len(steps),))],
        cost_estimate=pl.CostEstimate(
            flops=0, bytes_accessed=4 * row_count * columns * len(steps), transcendentals=0
        ),
        compiler_params=pltpu.CompilerParams(vmem_limit_bytes=8 * 1024 * 1024),
        name="join_columns",
    )(*args)


def finish(chunks, into, arrived, outer, momentum, live, scale):
    steps = list(chunks)
    row_count, columns = chunks[steps[0]].shape
    slot_count = arrived.shape[0]
    blocks = 8
    rows = slot_count // blocks

    def kernel(*refs):
        ins = refs[: len(steps)]
        arrived_ref, outer_ref, momentum_ref, live_ref, _ = refs[len(steps) : len(steps) + 5]
        new_outer_ref, new_momentum_ref, joined_ref, sems = refs[len(steps) + 5 :]
        i = pl.program_id(0)
        me = lax.axis_index("replica")
        copies = []
        for k, step in enumerate(steps):
            come = place_traced(me, step)
            copies.append(
                pltpu.make_async_copy(
                    ins[k],
                    joined_ref.at[:, pl.ds(pl.multiple_of(come * columns, 128), columns)],
                    sems.at[k],
                )
            )

        @pl.when(i == 0)
        def _():
            for copy in copies:
                copy.start()

        alive = live_ref[...] > 0.0
        at = pl.ds(pl.multiple_of(i * rows, rows), rows)
        for start in range(0, columns, 128):
            cols = pl.ds(start, 128)
            mean = arrived_ref[:, cols].astype(jnp.float32) * scale
            old = outer_ref[:, cols]
            pseudo_grad = jnp.where(alive, old - mean, 0.0)
            fresh = momentum_decay * momentum_ref[at, cols] + pseudo_grad
            new_momentum_ref[:, cols] = fresh
            new_outer_ref[:, cols] = old - outer_rate * (pseudo_grad + momentum_decay * fresh)

        @pl.when(i == blocks - 1)
        def _():
            for copy in copies:
                copy.wait()

    whole = pl.BlockSpec(memory_space=pltpu.VMEM)
    in_hbm = pl.BlockSpec(memory_space=pltpu.HBM)
    block = pl.BlockSpec((rows, columns), lambda i: (i, 0))
    return pl.pallas_call(
        kernel,
        grid=(blocks,),
        out_shape=[jax.ShapeDtypeStruct((slot_count, columns), jnp.float32)] * 2
        + [jax.ShapeDtypeStruct(into.shape, into.dtype)],
        in_specs=[whole] * len(steps)
        + [block, block, whole, pl.BlockSpec((rows, 128), lambda i: (i, 0)), in_hbm],
        out_specs=[block, block, in_hbm],
        input_output_aliases={len(steps) + 4: 2},
        scratch_shapes=[pltpu.SemaphoreType.DMA((len(steps),))],
        cost_estimate=pl.CostEstimate(
            flops=10 * slot_count * columns,
            bytes_accessed=4 * row_count * columns * len(steps) + 18 * slot_count * columns,
            transcendentals=0,
        ),
        compiler_params=pltpu.CompilerParams(vmem_limit_bytes=12 * 1024 * 1024),
        name="finish",
    )(
        *[chunks[step] for step in steps],
        arrived,
        pltpu.with_memory_space_constraint(outer, pltpu.HBM),
        momentum,
        live,
        into,
    )


def fresh_rows(parts, share, scale):
    row_count, columns = share.shape
    width = 256

    def kernel(*refs):
        part_refs = refs[: len(parts)]
        share_ref, rows_ref, total_ref = refs[len(parts) :]
        for start in range(0, columns, width):
            at = (slice(None), pl.ds(start, width))
            total = part_refs[0][at].astype(jnp.float32)
            for ref in part_refs[1:]:
                total = total + ref[at].astype(jnp.float32)
            more = share_ref[at].astype(jnp.float32)
            rows_ref[at] = (more + scale * total).astype(rows_ref.dtype)
            total_ref[at] = total.astype(total_ref.dtype)

    return pl.pallas_call(
        kernel,
        out_shape=[jax.ShapeDtypeStruct((row_count, columns), jnp.bfloat16)] * 2,
        in_specs=[pl.BlockSpec(memory_space=pltpu.VMEM)] * (len(parts) + 1),
        out_specs=[pl.BlockSpec(memory_space=pltpu.VMEM)] * 2,
        cost_estimate=pl.CostEstimate(
            flops=row_count * columns * (len(parts) + 2),
            bytes_accessed=2 * columns * row_count * (len(parts) + 3),
            transcendentals=0,
        ),
        compiler_params=pltpu.CompilerParams(vmem_limit_bytes=8 * 1024 * 1024),
        name="fresh_rows",
    )(*parts, share)


def partial_sums(*sums):
    row_count, columns = sums[0][0].shape
    width = 256

    def kernel(*refs):
        ins, outs = refs[: -len(sums)], refs[-len(sums) :]
        first = 0
        for terms, out in zip(sums, outs):
            term_refs = ins[first : first + len(terms)]
            first += len(terms)
            for start in range(0, columns, width):
                at = (slice(None), pl.ds(start, width))
                total = term_refs[0][at].astype(jnp.float32)
                for ref in term_refs[1:]:
                    total = total + ref[at].astype(jnp.float32)
                out[at] = total.astype(out.dtype)

    terms = [term for group in sums for term in group]
    return pl.pallas_call(
        kernel,
        out_shape=[jax.ShapeDtypeStruct((row_count, columns), jnp.bfloat16)] * len(sums),
        in_specs=[pl.BlockSpec(memory_space=pltpu.VMEM)] * len(terms),
        out_specs=[pl.BlockSpec(memory_space=pltpu.VMEM)] * len(sums),
        cost_estimate=pl.CostEstimate(
            flops=PACE,
            bytes_accessed=2 * columns * row_count * (len(terms) + len(sums)),
            transcendentals=0,
        ),
        compiler_params=pltpu.CompilerParams(vmem_limit_bytes=8 * 1024 * 1024),
        name="partial_sums",
    )(*terms)


def pick_rows(pick, array, name):
    count, columns = pick.shape[0], array.shape[1]
    width = 256

    def kernel(pick_ref, array_ref, out_ref):
        for start in range(0, columns, width):
            cols = pl.ds(start, width)
            out_ref[:, cols] = jnp.dot(
                pick_ref[...], array_ref[:, cols], preferred_element_type=jnp.float32
            ).astype(out_ref.dtype)

    return pl.pallas_call(
        kernel,
        out_shape=jax.ShapeDtypeStruct((count, columns), array.dtype),
        in_specs=[pl.BlockSpec(memory_space=pltpu.VMEM)] * 2,
        out_specs=pl.BlockSpec(memory_space=pltpu.VMEM),
        cost_estimate=pl.CostEstimate(
            flops=2 * count * array.shape[0] * columns,
            bytes_accessed=2 * columns * (count + array.shape[0]),
            transcendentals=0,
        ),
        compiler_params=pltpu.CompilerParams(vmem_limit_bytes=4 * 1024 * 1024),
        name=name,
    )(pick, array)


def gate(*arrays):
    def kernel(*refs):
        pass

    return pl.pallas_call(
        kernel,
        out_shape=[jax.ShapeDtypeStruct(array.shape, array.dtype) for array in arrays],
        in_specs=[pl.BlockSpec(memory_space=pl.ANY)] * len(arrays),
        out_specs=[pl.BlockSpec(memory_space=pl.ANY)] * len(arrays),
        input_output_aliases={i: i for i in range(len(arrays))},
        cost_estimate=pl.CostEstimate(flops=GATE_PACE, bytes_accessed=0, transcendentals=0),
        compiler_params=pltpu.CompilerParams(vmem_limit_bytes=1024 * 1024),
        name="gate",
    )(*arrays)


def sum_over_replica(rows):
    own = split_columns(rows)
    up_far = send(own[1, 1], (1, 0))
    down_far = send(own[3, 1], (3, 0))
    across = send(own[2, 1], (0, 1))
    up = send(own[1, 0], (1, 0))
    down = send(own[3, 0], (3, 0))
    for_twice, for_beside = partial_sums((own[2, 0], across), (own[0, 1], up_far, down_far))
    twice = send(for_twice, (2, 0))
    beside = send(for_beside, (0, 1))
    return (own[0, 0], up, down, twice, beside), for_beside


def gather_over_replica(rows):
    got = {(0, 0): rows}
    got[0, 1] = send(rows, (0, 1))
    got[2, 0] = send(rows, (2, 0))
    got[3, 0] = send(rows, (1, 0))
    got[1, 0] = send(rows, (3, 0))
    near, far = got[0, 1], got[2, 0] = gate(got[0, 1], got[2, 0])
    got[3, 1] = send(near, (1, 0))
    got[1, 1] = send(near, (3, 0))
    got[2, 1] = send(far, (0, 1))
    return got


def body(local_params, outer_params, outer_momentum, block_lengths, block_owners):
    fsdp_count = lax.axis_size("fsdp")
    group_count = lax.axis_size("replica")
    my_index = lax.axis_index("fsdp")
    own_rows = local_params[0]
    row_count = own_rows.shape[0]
    slots = outer_params.shape[2]
    columns = outer_params.shape[3]
    outer_here = outer_params[0]
    momentum_here = outer_momentum[0]

    parts, halfway = sum_over_replica(own_rows)

    base = (keep * outer_here - drag * momentum_here).astype(jnp.bfloat16)
    own_base = lax.all_to_all(base, "fsdp", split_axis=0, concat_axis=0, tiled=True)

    block_lengths, _ = lax.optimization_barrier((block_lengths, halfway))
    counts, starts = tables(block_lengths, block_owners, fsdp_count)
    slot_ids = jnp.arange(slots, dtype=jnp.int32)
    row_ids = jnp.arange(row_count, dtype=jnp.int32)
    my_starts = lax.dynamic_index_in_dim(starts, my_index, 0, keepdims=False)
    my_counts = lax.dynamic_index_in_dim(counts, my_index, 0, keepdims=False)
    incoming = lax.dynamic_index_in_dim(counts, my_index, 1, keepdims=False)
    live_in = (slot_ids[None, :] < incoming[:, None]).astype(jnp.float32).reshape(-1, 1)
    live_in = jnp.broadcast_to(live_in, (fsdp_count * slots, 128))
    row_of_slot = jnp.where(
        slot_ids[None, :] < my_counts[:, None], my_starts[:, None] + slot_ids[None, :], -1
    ).reshape(-1)
    pick = (row_of_slot[:, None] == row_ids[None, :]).astype(own_rows.dtype)
    unpick = (row_ids[:, None] == row_of_slot[None, :]).astype(own_rows.dtype)
    share = pick_rows(unpick, own_base.reshape(-1, columns), "own_share")
    rows, total = fresh_rows(parts, share, pull / group_count)
    packed = pick_rows(pick, total, "pack_slots")
    gathered = gather_over_replica(rows)
    arrived = lax.all_to_all(
        packed.reshape(fsdp_count, slots, columns), "fsdp", split_axis=0, concat_axis=0, tiled=True
    )
    flat = (fsdp_count * slots, columns)
    first = [(0, 0), (0, 1), (2, 0), (1, 0), (3, 0)]
    joined = join_columns({step: gathered[step] for step in first})
    fresh_outer, fresh_momentum, joined = finish(
        {step: gathered[step] for step in STEPS if step not in first},
        joined,
        arrived.reshape(flat),
        outer_here.reshape(flat),
        momentum_here.reshape(flat),
        live_in,
        1.0 / group_count,
    )
    return (
        fresh_outer.reshape(outer_params.shape),
        fresh_momentum.reshape(outer_params.shape),
        joined,
    )


def solution(mesh):
    in_specs = (
        P("replica", "fsdp", None),
        P("fsdp", None, None, "replica"),
        P("fsdp", None, None, "replica"),
        P(),
        P(),
    )
    out_specs = (
        P("fsdp", None, None, "replica"),
        P("fsdp", None, None, "replica"),
        P("fsdp", None),
    )
    return jax.shard_map(body, mesh=mesh, in_specs=in_specs, out_specs=out_specs, check_vma=False)
```
